32 devices in a mesh: prow: 4 (over x, core), pcol: 8 (over z, y).
Axes of the slice: x: 2, y: 2, z: 4, core: 2. Of those that a mesh axis runs over, the one named last changes fastest.
Arguments:
- inverse_blocks: bfloat16 [7168, 7168], P('prow', 'pcol'), may hold values from -6 to 6
- lower_late: bfloat16 [56, 128, 256], P('prow', 'pcol'), may hold values from -0.09375 to 0.09375
- lower_early: bfloat16 [56, 128, 256], P('prow', 'pcol'), may hold values from -0.09375 to 0.09375
- link_block: bfloat16 [256, 256], replicated, may hold values from -0.375 to 0.375
- diag_inverse: float32 [2, 256, 256], replicated, may hold values from -6 to 6
- structures: int32 [2, 28], replicated, may hold values from 0 to 55, as said below
Outputs:
- panel_late: float32 [56, 128, 256], P('prow', 'pcol')
- diag_late: float32 [256, 256], replicated
- panel_early: float32 [56, 128, 256], P('prow', 'pcol')
- cross_block: float32 [256, 256], replicated
- diag_early: float32 [256, 256], replicated
The draws below stay inside these ranges and needn't reach their ends.
Inputs may be any that keep to these rules, and one draw needn't show every extreme that they name: `structures`: each row lists 28 different block numbers in increasing order. Among the 14 blocks with the same value of n // 14 at most 10 are listed, and in each row some such group has exactly 10.
All inputs are finite; a program needn't handle non-finite values.
Results may differ from the reference program's by a relative error of at most 0.01.
Values may be sent and summed in bfloat16 or wider, within the bound.
A program may use at most 64 MiB of HBM per device.

```python
import jax
import jax.numpy as jnp
from jax import lax

WIDTH = 256
BLK = 128
BLK_DEV = 7
NBLK = 56
LISTED = 28
N_PCOL = 8


def one_structure(key):
    groups = NBLK // (2 * BLK_DEV)
    pairs = groups // 2
    key_order, key_shift, key_score = jax.random.split(key, 3)
    order_rows = jax.random.permutation(key_order, groups)
    shift = jax.random.randint(key_shift, (pairs,), 0, BLK_DEV // 2 + 1)
    shift = shift.at[0].set(BLK_DEV // 2)
    pair_counts = jnp.concatenate([BLK_DEV + shift, BLK_DEV - shift])
    counts = jnp.zeros((groups,), jnp.int32).at[order_rows].set(pair_counts.astype(jnp.int32))
    scores = jax.random.randint(key_score, (groups, 2 * BLK_DEV), 0, 1048576)
    scores = scores * (2 * BLK_DEV) + jnp.arange(2 * BLK_DEV, dtype=jnp.int32)[None, :]
    ranking = jnp.argsort(jnp.argsort(scores, axis=1), axis=1)
    chosen = (ranking < counts[:, None]).reshape(NBLK)
    sort_keys = jnp.where(chosen, 0, 1).astype(jnp.int32) * NBLK + jnp.arange(NBLK, dtype=jnp.int32)
    picked = jnp.argsort(sort_keys)[:LISTED]
    return jnp.sort(picked).astype(jnp.int32)


def draw_structures(key, part):
    first = one_structure(jax.random.fold_in(key, 11))
    second = one_structure(jax.random.fold_in(key, 23))
    return jnp.stack([first, second]).astype(jnp.int32)


def block_scale(key, shape, shards, least, largest):
    loudness = 1.0
    for position, shards_of in shards:
        draws = jax.random.uniform(jax.random.fold_in(jax.random.fold_in(key, 6), position), (shards_of,), jnp.float32, least / len(shards), largest / len(shards))
        loudness = loudness * jnp.repeat(jnp.exp(draws), shape[position] // shards_of).reshape((-1,) + (1,) * (len(shape) - 1 - position))
    return loudness


def noise(key, extent, deviation, bound, pieces=(), held_as=jnp.bfloat16):
    entries = jax.random.normal(key, extent, jnp.float32) * deviation
    if len(pieces) > 0:
        entries = block_scale(key, extent, pieces, -0.22, 0.18) * entries
    return jnp.clip(entries, min=-bound, max=bound).astype(held_as)


def setup_inputs(seed: int = 0) -> dict:
    key_of = jax.random.split(jax.random.key(seed), 7)
    return {
        "inverse_blocks": noise(key_of[0], (NBLK * BLK, NBLK * BLK), 1.0, 6.0, ((0, 4), (1, 8))),
        "lower_late": noise(key_of[1], (NBLK, BLK, WIDTH), (LISTED * BLK) ** -0.5, 0.09375, ((0, 4), (1, 8))),
        "lower_early": noise(key_of[2], (NBLK, BLK, WIDTH), (LISTED * BLK) ** -0.5, 0.09375, ((0, 4), (1, 8))),
        "link_block": noise(key_of[3], (WIDTH, WIDTH), WIDTH ** -0.5, 0.375),
        "diag_inverse": noise(key_of[4], (2, WIDTH, WIDTH), 1.0, 6.0, (), jnp.float32),
        "structures": draw_structures(jax.random.fold_in(key_of[6], 71), 0),
    }


def mask_of(listed):
    return jnp.zeros((NBLK,), jnp.float32).at[listed].set(1.0)


def reduced_panel(inverse_blocks, masked):
    flat = masked.reshape(NBLK * BLK, WIDTH)
    group_rows = BLK_DEV * BLK

    def add_group(group, total):
        start = (group * group_rows).astype(jnp.int32)
        columns = lax.dynamic_slice(inverse_blocks, (jnp.int32(0), start), (NBLK * BLK, group_rows)).astype(jnp.float32)
        rows = lax.dynamic_slice(flat, (start, jnp.int32(0)), (group_rows, WIDTH)).astype(jnp.float32)
        product = jnp.dot(columns, rows, precision=lax.Precision.HIGHEST)
        rounded = lax.optimization_barrier(product.astype(jnp.bfloat16))
        return total + rounded.astype(jnp.float32)

    total = lax.fori_loop(0, N_PCOL, add_group, jnp.zeros((NBLK * BLK, WIDTH), jnp.float32))
    return total.reshape(NBLK, BLK, WIDTH)


def reference(inverse_blocks, lower_late, lower_early, link_block, diag_inverse, structures):
    high = lax.Precision.HIGHEST
    mask_late = mask_of(structures[0])
    mask_early = mask_of(structures[1])
    masked_late = (lower_late.astype(jnp.float32) * mask_late[:, None, None]).astype(jnp.bfloat16)
    masked_early = (lower_early.astype(jnp.float32) * mask_early[:, None, None]).astype(jnp.bfloat16)
    reduced_late = reduced_panel(inverse_blocks, masked_late)
    reduced_early = reduced_panel(inverse_blocks, masked_early)
    link_float = link_block.astype(jnp.float32)
    late_rows = masked_late.reshape(NBLK * BLK, WIDTH).astype(jnp.float32)
    early_rows = masked_early.reshape(NBLK * BLK, WIDTH).astype(jnp.float32)
    panel_late = -(reduced_late * mask_late[:, None, None])
    late_flat = panel_late.reshape(NBLK * BLK, WIDTH)
    diag_late = diag_inverse[0] - jnp.dot(late_rows.T, late_flat, precision=high)
    carried = jnp.dot(late_flat, link_float, precision=high).reshape(NBLK, BLK, WIDTH)
    panel_early = -((reduced_early + carried) * mask_early[:, None, None])
    early_flat = panel_early.reshape(NBLK * BLK, WIDTH)
    cross_block = -jnp.dot(late_flat.T, early_rows, precision=high) - jnp.dot(diag_late, link_float, precision=high)
    diag_early = diag_inverse[1] - jnp.dot(early_rows.T, early_flat, precision=high) - jnp.dot(link_float.T, cross_block, precision=high)
    return (panel_late, diag_late, panel_early, cross_block, diag_early)
```

```python
import functools

import jax
import jax.numpy as jnp
from jax import lax
from jax.experimental import pallas as pl
from jax.experimental.pallas import tpu as pltpu
from jax.sharding import PartitionSpec as P

WIDTH = 256
BLK = 128


def from_root(value, axis, source):
    kept = jnp.where(lax.axis_index(axis) == source, value, 0).astype(value.dtype)
    return lax.psum(kept, axis)


def split_parts(values):
    upper = values.astype(jnp.bfloat16)
    lower = (values - upper.astype(jnp.float32)).astype(jnp.bfloat16)
    return (upper, lower)


def rows_product(left, right_float):
    upper, lower = split_parts(right_float)
    dims = (((0,), (0,)), ((), ()))
    first = lax.dot_general(left, upper, dims, preferred_element_type=jnp.float32)
    return first + lax.dot_general(left, lower, dims, preferred_element_type=jnp.float32)


def plain_shards(inverse_blocks, lower_late, lower_early, link_block, diag_inverse, structures):
    high = lax.Precision.HIGHEST
    row_blocks = inverse_blocks.shape[0] // BLK
    col_blocks = inverse_blocks.shape[1] // BLK
    row_id = lax.axis_index("prow")
    col_id = lax.axis_index("pcol")
    block_ids = row_id * row_blocks + jnp.arange(row_blocks, dtype=jnp.int32)

    def block_hits(listed):
        return jnp.any(listed[:, None] == block_ids[None, :], axis=0).astype(jnp.float32)

    def own_columns(strip):
        return lax.dynamic_slice_in_dim(strip, col_id % 2 * col_blocks, col_blocks, 0)

    def reduce_columns(columns, flag_list):
        count = len(flag_list)
        product = jnp.dot(inverse_blocks, columns, preferred_element_type=jnp.float32)
        summed = lax.psum_scatter(
            product.reshape(row_blocks, BLK, count * WIDTH).astype(jnp.bfloat16),
            "pcol",
            scatter_dimension=1,
            tiled=True,
        ).astype(jnp.float32)
        return [summed]

    def separate_reduce(masked, hit_flags):
        strip = lax.all_gather(masked, "pcol", axis=1, tiled=True)
        columns = from_root(own_columns(strip), "prow", col_id // 2)
        columns = columns.reshape(col_blocks * BLK, WIDTH)
        return reduce_columns(columns, [hit_flags])[0]

    hits_late = block_hits(structures[0])
    hits_early = block_hits(structures[1])
    masked_late = lower_late * hits_late.astype(jnp.bfloat16)[:, None, None]
    masked_early = lower_early * hits_early.astype(jnp.bfloat16)[:, None, None]
    late_rows = masked_late.reshape(-1, WIDTH)
    early_rows = masked_early.reshape(-1, WIDTH)
    link_float = link_block.astype(jnp.float32)
    reduced_late = separate_reduce(masked_late, hits_late)
    reduced_early = separate_reduce(masked_early, hits_early)
    panel_late = -(reduced_late * hits_late[:, None, None])
    late_flat = panel_late.reshape(-1, WIDTH)
    local_late = rows_product(late_rows, late_flat)
    cross_local = rows_product(early_rows, late_flat).T
    sum_late = lax.psum(local_late, ("prow", "pcol"))
    diag_late = diag_inverse[0] - sum_late
    flat_upper, flat_lower = split_parts(late_flat)
    carried = jnp.dot(flat_upper, link_block, preferred_element_type=jnp.float32) + jnp.dot(
        flat_lower, link_block, preferred_element_type=jnp.float32
    )
    panel_early = -(
        (reduced_early + carried.reshape(reduced_early.shape)) * hits_early[:, None, None]
    )
    local_early = rows_product(early_rows, panel_early.reshape(-1, WIDTH))
    sum_early, cross_sum = lax.psum((local_early, cross_local), ("prow", "pcol"))
    cross_block = -cross_sum - jnp.dot(diag_late, link_float, precision=high)
    diag_early = diag_inverse[1] - sum_early - jnp.dot(link_float.T, cross_block, precision=high)
    return (panel_late, diag_late, panel_early, cross_block, diag_early)


GRID_ROWS = 4
GRID_COLS = 8
DEPTH = 4
MOST = 10
SPARE = 4
LANES = 128
F32 = jnp.float32
BF16 = jnp.bfloat16
MESH = pl.DeviceIdType.MESH


def fits_kernel(mesh, inverse_blocks, lower_late):
    sizes = (mesh.shape["prow"], mesh.shape["pcol"])
    return (
        sizes == (GRID_ROWS, GRID_COLS)
        and lower_late.shape == (14, BLK // GRID_COLS, WIDTH)
        and inverse_blocks.shape == (14 * BLK, 7 * BLK)
    )


def turned(left, right):
    return lax.dot_general(left, right, (((0,), (0,)), ((), ())), preferred_element_type=F32)


def step_kernel(
    inverse_hbm, late_ref, early_ref, link_ref, diag_ref, structures_ref,
    panel_late_ref, diag_late_ref, panel_early_ref, cross_ref, diag_early_ref,
    inverse, masked, columns, wide, product, from_y, to_z, from_z, summed,
    sums, sums_wide, plane_in, depth_in, totals,
    inverse_sem, first_send, first_recv, core_send, core_recv, x_send, x_recv,
    relay_send, relay_recv, y_send, y_recv, z_send, z_recv,
    plane_send, plane_recv, depth_send, depth_recv, total_send, total_recv,
):
    row_id = lax.axis_index("prow")
    col_id = lax.axis_index("pcol")
    z_id = col_id // 2
    y_id = lax.rem(col_id, 2)
    blocks, rows, _ = late_ref.shape
    half = blocks // 2
    listed = structures_ref.shape[1]
    core_peer = row_id + 1 - 2 * lax.rem(row_id, 2)
    x_peer = lax.rem(row_id + 2, GRID_ROWS)

    inverse_copy = pltpu.make_async_copy(inverse_hbm, inverse, inverse_sem)
    inverse_copy.start()

    barrier = pltpu.get_barrier_semaphore()
    for step in range(1, GRID_ROWS * GRID_COLS):
        other = lax.rem(row_id * GRID_COLS + col_id + step, GRID_ROWS * GRID_COLS)
        pl.semaphore_signal(
            barrier,
            inc=1,
            device_id=(other // GRID_COLS, lax.rem(other, GRID_COLS)),
            device_id_type=MESH,
        )

    hits, kept, dropped = [], [], []
    for panel in range(2):
        lowest = row_id * blocks
        entries = [structures_ref[panel, entry] - lowest for entry in range(listed)]
        unlisted = jnp.int32(0)
        panel_hits, panel_kept, panel_dropped = [], [], []
        for block in range(blocks):
            hit = jnp.int32(0)
            for entry in entries:
                hit += (entry == block).astype(jnp.int32)
            drop = (1 - hit) * (unlisted < SPARE).astype(jnp.int32)
            panel_hits.append(hit.astype(F32))
            panel_kept.append(1 - drop)
            panel_dropped.append(jnp.minimum(unlisted, SPARE))
            unlisted += 1 - hit
        hits.append(panel_hits)
        kept.append(panel_kept)
        dropped.append(panel_dropped)

    def weight(panel, block, shift):
        same = (dropped[panel][block] == shift).astype(jnp.int32)
        return (same * kept[panel][block]).astype(F32)

    def placed(panel, block):
        parts = [
            weight(panel, block, shift) * summed[panel, block - shift]
            for shift in range(SPARE + 1)
            if 0 <= block - shift < MOST
        ]
        return functools.reduce(jnp.add, parts)

    for panel, source in enumerate((late_ref, early_ref)):
        for block in range(blocks):
            masked[block, :, panel * WIDTH : (panel + 1) * WIDTH] = (
                source[block].astype(F32) * hits[panel][block]
            ).astype(BF16)

    pl.semaphore_wait(barrier, GRID_ROWS * GRID_COLS - 1)

    def remote(source, target, send, recv, device):
        return pltpu.make_async_remote_copy(
            src_ref=source,
            dst_ref=target,
            send_sem=send,
            recv_sem=recv,
            device_id=device,
            device_id_type=MESH,
        )

    def lanes(of_row):
        return pl.ds(pl.multiple_of(of_row * LANES, LANES), LANES)

    def first_copy(quarter, y_to):
        return remote(
            masked.at[y_to * half : (y_to + 1) * half, :, quarter * LANES : (quarter + 1) * LANES],
            columns.at[:, col_id, :, quarter * LANES : (quarter + 1) * LANES],
            first_send.at[quarter * 2 + y_to],
            first_recv.at[col_id],
            (jnp.int32(quarter), row_id * 2 + y_to),
        )

    def own_copy(quarter, y_to):
        return pltpu.make_async_copy(
            masked.at[y_to * half : (y_to + 1) * half, :, quarter * LANES : (quarter + 1) * LANES],
            columns.at[:, col_id, :, quarter * LANES : (quarter + 1) * LANES],
            first_recv.at[col_id],
        )

    def is_self(quarter, y_to):
        return (row_id == quarter) & (col_id == row_id * 2 + y_to)

    for quarter in range(GRID_ROWS):
        for y_to in range(2):
            pl.when(jnp.logical_not(is_self(quarter, y_to)))(first_copy(quarter, y_to).start)
            pl.when(is_self(quarter, y_to))(own_copy(quarter, y_to).start)

    def strip(source, of_row):
        return columns.at[:, source, :, lanes(of_row)]

    def core_copy(source):
        part = strip(source, row_id)
        return remote(part, part, core_send.at[source], core_recv.at[source], (core_peer, col_id))

    def x_copy(source):
        part = strip(source, row_id)
        return remote(part, part, x_send.at[source], x_recv.at[source], (x_peer, col_id))

    def relay_copy(source):
        part = strip(source, x_peer)
        return remote(part, part, relay_send.at[source], relay_recv.at[source], (core_peer, col_id))

    def arrived(part, sem):
        pltpu.make_async_copy(part, part, sem).wait()

    for source in range(GRID_COLS):
        arrived(strip(source, row_id), first_recv.at[source])
        x_copy(source).start()
        core_copy(source).start()
    for source in range(GRID_COLS):
        arrived(strip(source, x_peer), x_recv.at[source])
        relay_copy(source).start()
    core_other = lax.rem(core_peer + 2, GRID_ROWS)
    for source in range(GRID_COLS):
        arrived(strip(source, core_peer), core_recv.at[source])
        arrived(strip(source, core_other), relay_recv.at[source])
    inverse_copy.wait()

    def y_copy(panel, step):
        z_to = lax.rem(z_id + step, DEPTH)
        return remote(
            product.at[panel, :, z_to * 2 + 1 - y_id],
            from_y.at[panel, step],
            y_send.at[panel * DEPTH + step],
            y_recv.at[panel * DEPTH + step],
            (row_id, z_id * 2 + 1 - y_id),
        )

    def z_copy(panel, step):
        z_to = lax.rem(z_id + step, DEPTH)
        return remote(
            to_z.at[panel, step],
            from_z.at[panel, step],
            z_send.at[panel * DEPTH + step],
            z_recv.at[panel * DEPTH + step],
            (row_id, z_to * 2 + y_id),
        )

    order = (1, 2, 3, 0)
    for panel in range(2):
        right = columns[:, :, :, panel * WIDTH : (panel + 1) * WIDTH].reshape(-1, WIDTH)
        for start in range(0, blocks * BLK, 2 * BLK):
            wide[start : start + 2 * BLK] = jnp.dot(
                inverse[start : start + 2 * BLK], right, preferred_element_type=F32
            )
        for slot in range(MOST):
            chosen = functools.reduce(
                jnp.add,
                [
                    weight(panel, slot + shift, shift)
                    * wide[(slot + shift) * BLK : (slot + shift + 1) * BLK]
                    for shift in range(SPARE + 1)
                ],
            )
            product[panel, slot] = chosen.astype(BF16).reshape(GRID_COLS, rows, WIDTH)
        for step in order:
            y_copy(panel, step).start()

    for panel in range(2):
        for step in order[:-1]:
            y_copy(panel, step).wait_recv()
            z_to = lax.rem(z_id + step, DEPTH)
            to_z[panel, step] = (
                product[panel, :, z_to * 2 + y_id].astype(F32) + from_y[panel, step].astype(F32)
            ).astype(BF16)
            z_copy(panel, step).start()

    def finish(panel):
        y_copy(panel, 0).wait_recv()
        total = product[panel, :, z_id * 2 + y_id].astype(F32) + from_y[panel, 0].astype(F32)
        for step in range(1, DEPTH):
            z_copy(panel, step).wait_recv()
            total += from_z[panel, step].astype(F32)
        summed[panel] = total

    place_id = row_id * 2 + y_id
    peers = GRID_ROWS * 2
    piece = (2 * WIDTH // peers, WIDTH // peers)
    base = (0, 2 * WIDTH)

    def plane_device(step):
        other = lax.rem(place_id + step, peers)
        return other, (other // 2, z_id * 2 + lax.rem(other, 2))

    def part_of(stage, index):
        size = piece[stage]
        return pl.ds(pl.multiple_of(base[stage] + index * size, size), size)

    def plane_copy(stage, step):
        other, device = plane_device(step)
        return remote(
            sums.at[part_of(stage, other)],
            plane_in.at[step, base[stage] // peers : base[stage] // peers + piece[stage]],
            plane_send.at[stage * peers + step],
            plane_recv.at[stage * peers + step],
            device,
        )

    def depth_copy(stage, step):
        z_to = lax.rem(z_id + step, DEPTH)
        part = depth_in.at[z_id, base[stage] // peers : base[stage] // peers + piece[stage]]
        return remote(
            part,
            part,
            depth_send.at[stage * DEPTH + step],
            depth_recv.at[stage * DEPTH + step],
            (row_id, z_to * 2 + y_id),
        )

    def total_copy(stage, step):
        _, device = plane_device(step)
        part = totals.at[part_of(stage, place_id)]
        return remote(
            part,
            part,
            total_send.at[stage * peers + step],
            total_recv.at[stage * peers + step],
            device,
        )

    def store_sums(stage, value, at):
        sums_wide[at : at + WIDTH] = value
        sums[at : at + WIDTH] = value.astype(BF16)

    def plane_sum(stage):
        start = base[stage] // peers
        total = sums_wide[part_of(stage, place_id)]
        for step in range(1, peers):
            plane_copy(stage, step).wait_recv()
            total += plane_in[step, start : start + piece[stage]].astype(F32)
        depth_in[z_id, start : start + piece[stage]] = total.astype(BF16)
        for step in range(1, DEPTH):
            depth_copy(stage, step).start()

    def depth_sum(stage):
        start = base[stage] // peers
        for step in range(1, DEPTH):
            source = lax.rem(z_id + DEPTH - step, DEPTH)
            arrived(
                depth_in.at[source, start : start + piece[stage]],
                depth_recv.at[stage * DEPTH + step],
            )
        total = depth_in[0, start : start + piece[stage]].astype(F32)
        for source in range(1, DEPTH):
            total += depth_in[source, start : start + piece[stage]].astype(F32)
        totals[part_of(stage, place_id)] = total.astype(BF16)
        for step in range(1, peers):
            total_copy(stage, step).start()

    def gather_totals(stage):
        for step in range(1, peers):
            source = lax.rem(place_id + peers - step, peers)
            arrived(totals.at[part_of(stage, source)], total_recv.at[stage * peers + step])

    link = link_ref[...]
    late_rows = masked[:, :, :WIDTH].reshape(-1, WIDTH)
    early_rows = masked[:, :, WIDTH:].reshape(-1, WIDTH)

    finish(0)
    for block in range(blocks):
        panel_late_ref[block] = -(placed(0, block) * hits[0][block])
    late_flat = panel_late_ref[...].reshape(-1, WIDTH)
    upper, lower = split_parts(late_flat)
    store_sums(0, turned(late_rows, upper) + turned(late_rows, lower), 0)
    store_sums(0, turned(upper, early_rows) + turned(lower, early_rows), WIDTH)
    for step in range(1, peers):
        plane_copy(0, step).start()
    carried = jnp.dot(upper, link, preferred_element_type=F32) + jnp.dot(
        lower, link, preferred_element_type=F32
    )
    carried = carried.reshape(blocks, rows, WIDTH)

    finish(1)
    for block in range(blocks):
        panel_early_ref[block] = -(
            (placed(1, block) + carried[block]) * hits[1][block]
        )
    early_upper, early_lower = split_parts(panel_early_ref[...].reshape(-1, WIDTH))
    store_sums(1, turned(early_rows, early_upper) + turned(early_rows, early_lower), 2 * WIDTH)
    for step in range(1, peers):
        plane_copy(1, step).start()

    plane_sum(0)
    plane_sum(1)
    depth_sum(0)
    depth_sum(1)
    gather_totals(0)
    diag_late = diag_ref[0] - totals[:WIDTH].astype(F32)
    diag_late_ref[...] = diag_late
    upper, lower = split_parts(diag_late)
    cross = (
        -totals[WIDTH : 2 * WIDTH].astype(F32)
        - jnp.dot(upper, link, preferred_element_type=F32)
        - jnp.dot(lower, link, preferred_element_type=F32)
    )
    cross_ref[...] = cross
    upper, lower = split_parts(cross)
    carried = turned(link, upper) + turned(link, lower)
    gather_totals(1)
    diag_early_ref[...] = diag_ref[1] - totals[2 * WIDTH :].astype(F32) - carried

    for quarter in range(GRID_ROWS):
        for y_to in range(2):
            pl.when(jnp.logical_not(is_self(quarter, y_to)))(first_copy(quarter, y_to).wait_send)
    for source in range(GRID_COLS):
        x_copy(source).wait_send()
        core_copy(source).wait_send()
        relay_copy(source).wait_send()
    for panel in range(2):
        for step in range(DEPTH):
            y_copy(panel, step).wait_send()
        for step in range(1, DEPTH):
            z_copy(panel, step).wait_send()
            depth_copy(panel, step).wait_send()
        for step in range(1, peers):
            plane_copy(panel, step).wait_send()
            total_copy(panel, step).wait_send()


def kernel_shards(inverse_blocks, lower_late, lower_early, link_block, diag_inverse, structures):
    blocks, rows, _ = lower_late.shape
    dma = pltpu.SemaphoreType.DMA
    vmem = pl.BlockSpec(memory_space=pltpu.VMEM)
    square = jax.ShapeDtypeStruct((WIDTH, WIDTH), F32)
    panel = jax.ShapeDtypeStruct(lower_late.shape, F32)
    peers = GRID_ROWS * 2
    sized = pltpu.VMEM
    return pl.pallas_call(
        step_kernel,
        out_shape=(panel, square, panel, square, square),
        in_specs=[
            pl.BlockSpec(memory_space=pl.ANY),
            vmem,
            vmem,
            vmem,
            vmem,
            pl.BlockSpec(memory_space=pltpu.SMEM),
        ],
        out_specs=(vmem,) * 5,
        scratch_shapes=[
            sized(inverse_blocks.shape, BF16),
            sized((blocks, rows, 2 * WIDTH), BF16),
            sized((blocks // 2, GRID_COLS, rows, 2 * WIDTH), BF16),
            sized((blocks * BLK, WIDTH), F32),
            sized((2, MOST, GRID_COLS, rows, WIDTH), BF16),
            sized((2, DEPTH, MOST, rows, WIDTH), BF16),
            sized((2, DEPTH, MOST, rows, WIDTH), BF16),
            sized((2, DEPTH, MOST, rows, WIDTH), BF16),
            sized((2, MOST, rows, WIDTH), F32),
            sized((3 * WIDTH, WIDTH), BF16),
            sized((3 * WIDTH, WIDTH), F32),
            sized((peers, 3 * WIDTH // peers, WIDTH), BF16),
            sized((DEPTH, 3 * WIDTH // peers, WIDTH), BF16),
            sized((3 * WIDTH, WIDTH), BF16),
            dma,
            dma((GRID_ROWS * 2,)),
            dma((GRID_COLS,)),
            dma((GRID_COLS,)),
            dma((GRID_COLS,)),
            dma((GRID_COLS,)),
            dma((GRID_COLS,)),
            dma((GRID_COLS,)),
            dma((GRID_COLS,)),
            dma((2 * DEPTH,)),
            dma((2 * DEPTH,)),
            dma((2 * DEPTH,)),
            dma((2 * DEPTH,)),
            dma((2 * peers,)),
            dma((2 * peers,)),
            dma((2 * DEPTH,)),
            dma((2 * DEPTH,)),
            dma((2 * peers,)),
            dma((2 * peers,)),
        ],
        compiler_params=pltpu.CompilerParams(
            collective_id=0, has_side_effects=True, vmem_limit_bytes=40 * 1024 * 1024
        ),
    )(inverse_blocks, lower_late, lower_early, link_block, diag_inverse, structures)


def solution(mesh):
    placed = (P("prow", "pcol"), P("prow", "pcol", None), P("prow", "pcol", None), P(), P(), P())

    def shards(inverse_blocks, lower_late, *others):
        if fits_kernel(mesh, inverse_blocks, lower_late):
            return kernel_shards(inverse_blocks, lower_late, *others)
        return plain_shards(inverse_blocks, lower_late, *others)

    return jax.shard_map(
        shards,
        mesh=mesh,
        in_specs=placed,
        out_specs=(P("prow", "pcol", None), P(), P("prow", "pcol", None), P(), P()),
        check_vma=False,
    )
```

```python
import functools

import jax
import jax.numpy as jnp
from jax import lax
from jax.experimental import pallas as pl
from jax.experimental.pallas import tpu as pltpu
from jax.sharding import PartitionSpec as P

WIDTH = 256
BLK = 128


def from_root(value, axis, source):
    kept = jnp.where(lax.axis_index(axis) == source, value, 0).astype(value.dtype)
    return lax.psum(kept, axis)


def split_parts(values):
    upper = values.astype(jnp.bfloat16)
    lower = (values - upper.astype(jnp.float32)).astype(jnp.bfloat16)
    return (upper, lower)


def rows_product(left, right_float):
    upper, lower = split_parts(right_float)
    dims = (((0,), (0,)), ((), ()))
    first = lax.dot_general(left, upper, dims, preferred_element_type=jnp.float32)
    return first + lax.dot_general(left, lower, dims, preferred_element_type=jnp.float32)


def plain_shards(inverse_blocks, lower_late, lower_early, link_block, diag_inverse, structures):
    high = lax.Precision.HIGHEST
    row_blocks = inverse_blocks.shape[0] // BLK
    col_blocks = inverse_blocks.shape[1] // BLK
    row_id = lax.axis_index("prow")
    col_id = lax.axis_index("pcol")
    block_ids = row_id * row_blocks + jnp.arange(row_blocks, dtype=jnp.int32)

    def block_hits(listed):
        return jnp.any(listed[:, None] == block_ids[None, :], axis=0).astype(jnp.float32)

    def own_columns(strip):
        return lax.dynamic_slice_in_dim(strip, col_id % 2 * col_blocks, col_blocks, 0)

    def reduce_columns(columns, flag_list):
        count = len(flag_list)
        product = jnp.dot(inverse_blocks, columns, preferred_element_type=jnp.float32)
        summed = lax.psum_scatter(
            product.reshape(row_blocks, BLK, count * WIDTH).astype(jnp.bfloat16),
            "pcol",
            scatter_dimension=1,
            tiled=True,
        ).astype(jnp.float32)
        return [summed]

    def separate_reduce(masked, hit_flags):
        strip = lax.all_gather(masked, "pcol", axis=1, tiled=True)
        columns = from_root(own_columns(strip), "prow", col_id // 2)
        columns = columns.reshape(col_blocks * BLK, WIDTH)
        return reduce_columns(columns, [hit_flags])[0]

    hits_late = block_hits(structures[0])
    hits_early = block_hits(structures[1])
    masked_late = lower_late * hits_late.astype(jnp.bfloat16)[:, None, None]
    masked_early = lower_early * hits_early.astype(jnp.bfloat16)[:, None, None]
    late_rows = masked_late.reshape(-1, WIDTH)
    early_rows = masked_early.reshape(-1, WIDTH)
    link_float = link_block.astype(jnp.float32)
    reduced_late = separate_reduce(masked_late, hits_late)
    reduced_early = separate_reduce(masked_early, hits_early)
    panel_late = -(reduced_late * hits_late[:, None, None])
    late_flat = panel_late.reshape(-1, WIDTH)
    local_late = rows_product(late_rows, late_flat)
    cross_local = rows_product(early_rows, late_flat).T
    sum_late = lax.psum(local_late, ("prow", "pcol"))
    diag_late = diag_inverse[0] - sum_late
    flat_upper, flat_lower = split_parts(late_flat)
    carried = jnp.dot(flat_upper, link_block, preferred_element_type=jnp.float32) + jnp.dot(
        flat_lower, link_block, preferred_element_type=jnp.float32
    )
    panel_early = -(
        (reduced_early + carried.reshape(reduced_early.shape)) * hits_early[:, None, None]
    )
    local_early = rows_product(early_rows, panel_early.reshape(-1, WIDTH))
    sum_early, cross_sum = lax.psum((local_early, cross_local), ("prow", "pcol"))
    cross_block = -cross_sum - jnp.dot(diag_late, link_float, precision=high)
    diag_early = diag_inverse[1] - sum_early - jnp.dot(link_float.T, cross_block, precision=high)
    return (panel_late, diag_late, panel_early, cross_block, diag_early)


GRID_ROWS = 4
GRID_COLS = 8
DEPTH = 4
MOST = 10
SPARE = 4
LANES = 128
F32 = jnp.float32
BF16 = jnp.bfloat16
MESH = pl.DeviceIdType.MESH


def fits_kernel(mesh, inverse_blocks, lower_late):
    sizes = (mesh.shape["prow"], mesh.shape["pcol"])
    return (
        sizes == (GRID_ROWS, GRID_COLS)
        and lower_late.shape == (14, BLK // GRID_COLS, WIDTH)
        and inverse_blocks.shape == (14 * BLK, 7 * BLK)
    )


def turned(left, right):
    return lax.dot_general(left, right, (((0,), (0,)), ((), ())), preferred_element_type=F32)


def step_kernel(
    inverse_hbm, late_hbm, early_hbm, link_hbm, diag_hbm, structures_ref,
    panel_late_ref, diag_late_ref, panel_early_ref, cross_ref, diag_early_ref,
    inverse, late_ref, early_ref, link_ref, diag_ref, masked, columns, wide, product, from_y, to_z, from_z, summed,
    sums, sums_wide, plane_in, depth_in, totals,
    late_sem, early_sem, inverse_sem, link_sem, diag_sem, first_send, first_recv, core_send, core_recv, x_send, x_recv,
    relay_send, relay_recv, y_send, y_recv, z_send, z_recv,
    plane_send, plane_recv, depth_send, depth_recv, total_send, total_recv,
):
    row_id = lax.axis_index("prow")
    col_id = lax.axis_index("pcol")
    z_id = col_id // 2
    y_id = lax.rem(col_id, 2)
    blocks, rows, _ = late_ref.shape
    half = blocks // 2
    listed = structures_ref.shape[1]
    core_peer = row_id + 1 - 2 * lax.rem(row_id, 2)
    x_peer = lax.rem(row_id + 2, GRID_ROWS)

    late_copy = pltpu.make_async_copy(late_hbm, late_ref, late_sem)
    early_copy = pltpu.make_async_copy(early_hbm, early_ref, early_sem)
    inverse_copy = pltpu.make_async_copy(inverse_hbm, inverse, inverse_sem)
    link_copy = pltpu.make_async_copy(link_hbm, link_ref, link_sem)
    diag_copy = pltpu.make_async_copy(diag_hbm, diag_ref, diag_sem)
    for copy in (late_copy, early_copy, inverse_copy, link_copy, diag_copy):
        copy.start()

    barrier = pltpu.get_barrier_semaphore()
    for step in range(1, GRID_ROWS * GRID_COLS):
        other = lax.rem(row_id * GRID_COLS + col_id + step, GRID_ROWS * GRID_COLS)
        pl.semaphore_signal(
            barrier,
            inc=1,
            device_id=(other // GRID_COLS, lax.rem(other, GRID_COLS)),
            device_id_type=MESH,
        )

    hits = []
    for panel in range(2):
        entries = [structures_ref[panel, entry] - row_id * blocks for entry in range(listed)]
        panel_hits = []
        for block in range(blocks):
            hit = jnp.int32(0)
            for entry in entries:
                hit += (entry == block).astype(jnp.int32)
            panel_hits.append(hit)
        hits.append(panel_hits)

    late_copy.wait()
    early_copy.wait()
    for panel, source in enumerate((late_ref, early_ref)):
        for block in range(blocks):
            masked[block, :, panel * WIDTH : (panel + 1) * WIDTH] = (
                source[block].astype(F32) * hits[panel][block].astype(F32)
            ).astype(BF16)

    pl.semaphore_wait(barrier, GRID_ROWS * GRID_COLS - 1)

    def remote(source, target, send, recv, device):
        return pltpu.make_async_remote_copy(
            src_ref=source,
            dst_ref=target,
            send_sem=send,
            recv_sem=recv,
            device_id=device,
            device_id_type=MESH,
        )

    core_id = lax.rem(row_id, 2)
    x_id = row_id // 2

    def strip(panel, source, x_half):
        start = pl.multiple_of(panel * WIDTH + x_half * LANES, LANES)
        return columns.at[:, source, :, pl.ds(start, LANES)]

    def first_parts(panel, x_half, y_to):
        start = panel * WIDTH + x_half * LANES
        part = masked.at[y_to * half : (y_to + 1) * half, :, start : start + LANES]
        target = (x_half * 2 + lax.rem(y_id + panel, 2), row_id * 2 + y_to)
        at_self = (row_id == target[0]) & (col_id == target[1])
        return part, strip(panel, col_id, x_half), target, at_self

    def first_copy(panel, x_half, y_to):
        part, to, target, _ = first_parts(panel, x_half, y_to)
        send = first_send.at[panel * 4 + x_half * 2 + y_to]
        return remote(part, to, send, first_recv.at[panel * DEPTH + z_id], target)

    def own_copy(panel, x_half, y_to):
        part, to, _, _ = first_parts(panel, x_half, y_to)
        return pltpu.make_async_copy(part, to, first_recv.at[panel * DEPTH + z_id])

    def is_self(panel, x_half, y_to):
        return first_parts(panel, x_half, y_to)[3]

    first_cases = [(p, x, y) for p in range(2) for x in range(2) for y in range(2)]
    for case in first_cases:
        pl.when(jnp.logical_not(is_self(*case)))(first_copy(*case).start)
        pl.when(is_self(*case))(own_copy(*case).start)

    def here(panel, index):
        return index * 2 + lax.rem(core_id + panel, 2)

    def there(panel, index):
        return index * 2 + lax.rem(core_id + panel + 1, 2)

    def core_copy(panel, index):
        part, at = strip(panel, here(panel, index), x_id), panel * DEPTH + index
        return remote(part, part, core_send.at[at], core_recv.at[at], (core_peer, col_id))

    def x_copy(panel, index):
        part, at = strip(panel, here(panel, index), x_id), panel * DEPTH + index
        return remote(part, part, x_send.at[at], x_recv.at[at], (x_peer, col_id))

    def relay_copy(panel, index):
        part, at = strip(panel, here(panel, index), 1 - x_id), panel * DEPTH + index
        return remote(part, part, relay_send.at[at], relay_recv.at[at], (core_peer, col_id))

    def arrived(part, sem):
        pltpu.make_async_copy(part, part, sem).wait()

    def spread(panel):
        for index in range(DEPTH):
            arrived(strip(panel, here(panel, index), x_id), first_recv.at[panel * DEPTH + index])
            x_copy(panel, index).start()
            core_copy(panel, index).start()

    def relay(panel):
        for index in range(DEPTH):
            arrived(strip(panel, here(panel, index), 1 - x_id), x_recv.at[panel * DEPTH + index])
            relay_copy(panel, index).start()

    def collect(panel):
        for index in range(DEPTH):
            at = panel * DEPTH + index
            arrived(strip(panel, there(panel, index), x_id), core_recv.at[at])
            arrived(strip(panel, there(panel, index), 1 - x_id), relay_recv.at[at])

    kept, dropped = [], []
    for panel in range(2):
        unlisted = jnp.int32(0)
        panel_kept, panel_dropped = [], []
        for block in range(blocks):
            drop = (1 - hits[panel][block]) * (unlisted < SPARE).astype(jnp.int32)
            panel_kept.append(1 - drop)
            panel_dropped.append(jnp.minimum(unlisted, SPARE))
            unlisted += 1 - hits[panel][block]
        kept.append(panel_kept)
        dropped.append(panel_dropped)

    def weight(panel, block, shift):
        same = (dropped[panel][block] == shift).astype(jnp.int32)
        return (same * kept[panel][block]).astype(F32)

    def placed(panel, block):
        parts = [
            weight(panel, block, shift) * summed[panel, block - shift]
            for shift in range(SPARE + 1)
            if 0 <= block - shift < MOST
        ]
        return functools.reduce(jnp.add, parts)

    def y_copy(panel, step):
        z_to = lax.rem(z_id + step, DEPTH)
        return remote(
            product.at[panel, :, z_to * 2 + 1 - y_id],
            from_y.at[panel, step],
            y_send.at[panel * DEPTH + step],
            y_recv.at[panel * DEPTH + step],
            (row_id, z_id * 2 + 1 - y_id),
        )

    def z_copy(panel, step):
        z_to = lax.rem(z_id + step, DEPTH)
        return remote(
            to_z.at[panel, step],
            from_z.at[panel, step],
            z_send.at[panel * DEPTH + step],
            z_recv.at[panel * DEPTH + step],
            (row_id, z_to * 2 + y_id),
        )

    order = (1, 2, 3, 0)

    def multiply(panel):
        right = columns[:, :, :, panel * WIDTH : (panel + 1) * WIDTH].reshape(-1, WIDTH)
        for start in range(0, blocks * BLK, 2 * BLK):
            wide[start : start + 2 * BLK] = jnp.dot(
                inverse[start : start + 2 * BLK], right, preferred_element_type=F32
            )
        for slot in range(MOST):
            chosen = functools.reduce(
                jnp.add,
                [
                    weight(panel, slot + shift, shift)
                    * wide[(slot + shift) * BLK : (slot + shift + 1) * BLK]
                    for shift in range(SPARE + 1)
                ],
            )
            product[panel, slot] = chosen.astype(BF16).reshape(GRID_COLS, rows, WIDTH)
        for step in order:
            y_copy(panel, step).start()

    def forward(panel, step):
        y_copy(panel, step).wait_recv()
        z_to = lax.rem(z_id + step, DEPTH)
        to_z[panel, step] = (
            product[panel, :, z_to * 2 + y_id].astype(F32) + from_y[panel, step].astype(F32)
        ).astype(BF16)
        z_copy(panel, step).start()

    def finish(panel):
        y_copy(panel, 0).wait_recv()
        total = product[panel, :, z_id * 2 + y_id].astype(F32) + from_y[panel, 0].astype(F32)
        for step in range(1, DEPTH):
            z_copy(panel, step).wait_recv()
            total += from_z[panel, step].astype(F32)
        summed[panel] = total

    place_id = row_id * 2 + y_id
    peers = GRID_ROWS * 2
    piece = (2 * WIDTH // peers, WIDTH // peers)
    base = (0, 2 * WIDTH)

    def plane_device(step):
        other = lax.rem(place_id + step, peers)
        return other, (other // 2, z_id * 2 + lax.rem(other, 2))

    def part_of(stage, index):
        size = piece[stage]
        return pl.ds(pl.multiple_of(base[stage] + index * size, size), size)

    def plane_copy(stage, step):
        other, device = plane_device(step)
        return remote(
            sums.at[part_of(stage, other)],
            plane_in.at[step, base[stage] // peers : base[stage] // peers + piece[stage]],
            plane_send.at[stage * peers + step],
            plane_recv.at[stage * peers + step],
            device,
        )

    def depth_copy(stage, step):
        z_to = lax.rem(z_id + step, DEPTH)
        part = depth_in.at[z_id, base[stage] // peers : base[stage] // peers + piece[stage]]
        return remote(
            part,
            part,
            depth_send.at[stage * DEPTH + step],
            depth_recv.at[stage * DEPTH + step],
            (row_id, z_to * 2 + y_id),
        )

    def total_copy(stage, step):
        _, device = plane_device(step)
        part = totals.at[part_of(stage, place_id)]
        return remote(
            part,
            part,
            total_send.at[stage * peers + step],
            total_recv.at[stage * peers + step],
            device,
        )

    def store_sums(stage, value, at):
        sums_wide[at : at + WIDTH] = value
        sums[at : at + WIDTH] = value.astype(BF16)

    def plane_sum(stage):
        start = base[stage] // peers
        total = sums_wide[part_of(stage, place_id)]
        for step in range(1, peers):
            plane_copy(stage, step).wait_recv()
            total += plane_in[step, start : start + piece[stage]].astype(F32)
        depth_in[z_id, start : start + piece[stage]] = total.astype(BF16)
        for step in range(1, DEPTH):
            depth_copy(stage, step).start()

    def depth_sum(stage):
        start = base[stage] // peers
        for step in range(1, DEPTH):
            source = lax.rem(z_id + DEPTH - step, DEPTH)
            arrived(
                depth_in.at[source, start : start + piece[stage]],
                depth_recv.at[stage * DEPTH + step],
            )
        total = depth_in[0, start : start + piece[stage]].astype(F32)
        for source in range(1, DEPTH):
            total += depth_in[source, start : start + piece[stage]].astype(F32)
        totals[part_of(stage, place_id)] = total.astype(BF16)
        for step in range(1, peers):
            total_copy(stage, step).start()

    def gather_totals(stage):
        for step in range(1, peers):
            source = lax.rem(place_id + peers - step, peers)
            arrived(totals.at[part_of(stage, source)], total_recv.at[stage * peers + step])

    link_copy.wait()
    diag_copy.wait()
    link = link_ref[...]
    late_rows = masked[:, :, :WIDTH].reshape(-1, WIDTH)
    early_rows = masked[:, :, WIDTH:].reshape(-1, WIDTH)

    spread(0)
    relay(0)
    collect(0)
    inverse_copy.wait()
    multiply(0)
    spread(1)
    forward(0, 1)
    relay(1)
    forward(0, 2)
    collect(1)
    multiply(1)
    forward(0, 3)

    finish(0)
    for block in range(blocks):
        panel_late_ref[block] = -(placed(0, block) * hits[0][block].astype(F32))
    late_flat = panel_late_ref[...].reshape(-1, WIDTH)
    upper, lower = split_parts(late_flat)
    store_sums(0, turned(late_rows, upper) + turned(late_rows, lower), 0)
    store_sums(0, turned(upper, early_rows) + turned(lower, early_rows), WIDTH)
    for step in range(1, peers):
        plane_copy(0, step).start()
    carried = jnp.dot(upper, link, preferred_element_type=F32) + jnp.dot(
        lower, link, preferred_element_type=F32
    )
    carried = carried.reshape(blocks, rows, WIDTH)

    for step in order[:-1]:
        forward(1, step)
    plane_sum(0)

    finish(1)
    for block in range(blocks):
        panel_early_ref[block] = -(
            (placed(1, block) + carried[block]) * hits[1][block].astype(F32)
        )
    early_upper, early_lower = split_parts(panel_early_ref[...].reshape(-1, WIDTH))
    store_sums(1, turned(early_rows, early_upper) + turned(early_rows, early_lower), 2 * WIDTH)
    for step in range(1, peers):
        plane_copy(1, step).start()

    depth_sum(0)
    plane_sum(1)
    depth_sum(1)
    gather_totals(0)
    diag_late = diag_ref[0] - totals[:WIDTH].astype(F32)
    diag_late_ref[...] = diag_late
    upper, lower = split_parts(diag_late)
    cross = (
        -totals[WIDTH : 2 * WIDTH].astype(F32)
        - jnp.dot(upper, link, preferred_element_type=F32)
        - jnp.dot(lower, link, preferred_element_type=F32)
    )
    cross_ref[...] = cross
    upper, lower = split_parts(cross)
    carried = turned(link, upper) + turned(link, lower)
    gather_totals(1)
    diag_early_ref[...] = diag_ref[1] - totals[2 * WIDTH :].astype(F32) - carried

    for case in first_cases:
        pl.when(jnp.logical_not(is_self(*case)))(first_copy(*case).wait_send)
    for panel in range(2):
        for index in range(DEPTH):
            x_copy(panel, index).wait_send()
            core_copy(panel, index).wait_send()
            relay_copy(panel, index).wait_send()
    for panel in range(2):
        for step in range(DEPTH):
            y_copy(panel, step).wait_send()
        for step in range(1, DEPTH):
            z_copy(panel, step).wait_send()
            depth_copy(panel, step).wait_send()
        for step in range(1, peers):
            plane_copy(panel, step).wait_send()
            total_copy(panel, step).wait_send()


def kernel_shards(inverse_blocks, lower_late, lower_early, link_block, diag_inverse, structures):
    blocks, rows, _ = lower_late.shape
    dma = pltpu.SemaphoreType.DMA
    vmem = pl.BlockSpec(memory_space=pltpu.VMEM)
    square = jax.ShapeDtypeStruct((WIDTH, WIDTH), F32)
    panel = jax.ShapeDtypeStruct(lower_late.shape, F32)
    peers = GRID_ROWS * 2
    sized = pltpu.VMEM
    return pl.pallas_call(
        step_kernel,
        out_shape=(panel, square, panel, square, square),
        in_specs=[
            *(pl.BlockSpec(memory_space=pl.ANY),) * 5,
            pl.BlockSpec(memory_space=pltpu.SMEM),
        ],
        out_specs=(vmem,) * 5,
        scratch_shapes=[
            sized(inverse_blocks.shape, BF16),
            sized(lower_late.shape, BF16),
            sized(lower_early.shape, BF16),
            sized(link_block.shape, BF16),
            sized(diag_inverse.shape, F32),
            sized((blocks, rows, 2 * WIDTH), BF16),
            sized((blocks // 2, GRID_COLS, rows, 2 * WIDTH), BF16),
            sized((blocks * BLK, WIDTH), F32),
            sized((2, MOST, GRID_COLS, rows, WIDTH), BF16),
            sized((2, DEPTH, MOST, rows, WIDTH), BF16),
            sized((2, DEPTH, MOST, rows, WIDTH), BF16),
            sized((2, DEPTH, MOST, rows, WIDTH), BF16),
            sized((2, MOST, rows, WIDTH), F32),
            sized((3 * WIDTH, WIDTH), BF16),
            sized((3 * WIDTH, WIDTH), F32),
            sized((peers, 3 * WIDTH // peers, WIDTH), BF16),
            sized((DEPTH, 3 * WIDTH // peers, WIDTH), BF16),
            sized((3 * WIDTH, WIDTH), BF16),
            dma,
            dma,
            dma,
            dma,
            dma,
            dma((GRID_ROWS * 2,)),
            dma((GRID_COLS,)),
            dma((GRID_COLS,)),
            dma((GRID_COLS,)),
            dma((GRID_COLS,)),
            dma((GRID_COLS,)),
            dma((GRID_COLS,)),
            dma((GRID_COLS,)),
            dma((2 * DEPTH,)),
            dma((2 * DEPTH,)),
            dma((2 * DEPTH,)),
            dma((2 * DEPTH,)),
            dma((2 * peers,)),
            dma((2 * peers,)),
            dma((2 * DEPTH,)),
            dma((2 * DEPTH,)),
            dma((2 * peers,)),
            dma((2 * peers,)),
        ],
        compiler_params=pltpu.CompilerParams(
            collective_id=0, has_side_effects=True, vmem_limit_bytes=52 * 1024 * 1024
        ),
    )(inverse_blocks, lower_late, lower_early, link_block, diag_inverse, structures)


def solution(mesh):
    placed = (P("prow", "pcol"), P("prow", "pcol", None), P("prow", "pcol", None), P(), P(), P())

    def shards(inverse_blocks, lower_late, *others):
        if fits_kernel(mesh, inverse_blocks, lower_late):
            return kernel_shards(inverse_blocks, lower_late, *others)
        return plain_shards(inverse_blocks, lower_late, *others)

    return jax.shard_map(
        shards,
        mesh=mesh,
        in_specs=placed,
        out_specs=(P("prow", "pcol", None), P(), P("prow", "pcol", None), P(), P()),
        check_vma=False,
    )
```

```python
import functools

import jax
import jax.numpy as jnp
from jax import lax
from jax.experimental import pallas as pl
from jax.experimental.pallas import tpu as pltpu
from jax.sharding import PartitionSpec as P

WIDTH = 256
BLK = 128


def from_root(value, axis, source):
    kept = jnp.where(lax.axis_index(axis) == source, value, 0).astype(value.dtype)
    return lax.psum(kept, axis)


def split_parts(values):
    upper = values.astype(jnp.bfloat16)
    lower = (values - upper.astype(jnp.float32)).astype(jnp.bfloat16)
    return (upper, lower)


def rows_product(left, right_float):
    upper, lower = split_parts(right_float)
    dims = (((0,), (0,)), ((), ()))
    first = lax.dot_general(left, upper, dims, preferred_element_type=jnp.float32)
    return first + lax.dot_general(left, lower, dims, preferred_element_type=jnp.float32)


def plain_shards(inverse_blocks, lower_late, lower_early, link_block, diag_inverse, structures):
    high = lax.Precision.HIGHEST
    row_blocks = inverse_blocks.shape[0] // BLK
    col_blocks = inverse_blocks.shape[1] // BLK
    row_id = lax.axis_index("prow")
    col_id = lax.axis_index("pcol")
    block_ids = row_id * row_blocks + jnp.arange(row_blocks, dtype=jnp.int32)

    def block_hits(listed):
        return jnp.any(listed[:, None] == block_ids[None, :], axis=0).astype(jnp.float32)

    def own_columns(strip):
        return lax.dynamic_slice_in_dim(strip, col_id % 2 * col_blocks, col_blocks, 0)

    def reduce_columns(columns, flag_list):
        count = len(flag_list)
        product = jnp.dot(inverse_blocks, columns, preferred_element_type=jnp.float32)
        summed = lax.psum_scatter(
            product.reshape(row_blocks, BLK, count * WIDTH).astype(jnp.bfloat16),
            "pcol",
            scatter_dimension=1,
            tiled=True,
        ).astype(jnp.float32)
        return [summed]

    def separate_reduce(masked, hit_flags):
        strip = lax.all_gather(masked, "pcol", axis=1, tiled=True)
        columns = from_root(own_columns(strip), "prow", col_id // 2)
        columns = columns.reshape(col_blocks * BLK, WIDTH)
        return reduce_columns(columns, [hit_flags])[0]

    hits_late = block_hits(structures[0])
    hits_early = block_hits(structures[1])
    masked_late = lower_late * hits_late.astype(jnp.bfloat16)[:, None, None]
    masked_early = lower_early * hits_early.astype(jnp.bfloat16)[:, None, None]
    late_rows = masked_late.reshape(-1, WIDTH)
    early_rows = masked_early.reshape(-1, WIDTH)
    link_float = link_block.astype(jnp.float32)
    reduced_late = separate_reduce(masked_late, hits_late)
    reduced_early = separate_reduce(masked_early, hits_early)
    panel_late = -(reduced_late * hits_late[:, None, None])
    late_flat = panel_late.reshape(-1, WIDTH)
    local_late = rows_product(late_rows, late_flat)
    cross_local = rows_product(early_rows, late_flat).T
    sum_late = lax.psum(local_late, ("prow", "pcol"))
    diag_late = diag_inverse[0] - sum_late
    flat_upper, flat_lower = split_parts(late_flat)
    carried = jnp.dot(flat_upper, link_block, preferred_element_type=jnp.float32) + jnp.dot(
        flat_lower, link_block, preferred_element_type=jnp.float32
    )
    panel_early = -(
        (reduced_early + carried.reshape(reduced_early.shape)) * hits_early[:, None, None]
    )
    local_early = rows_product(early_rows, panel_early.reshape(-1, WIDTH))
    sum_early, cross_sum = lax.psum((local_early, cross_local), ("prow", "pcol"))
    cross_block = -cross_sum - jnp.dot(diag_late, link_float, precision=high)
    diag_early = diag_inverse[1] - sum_early - jnp.dot(link_float.T, cross_block, precision=high)
    return (panel_late, diag_late, panel_early, cross_block, diag_early)


GRID_ROWS = 4
GRID_COLS = 8
DEPTH = 4
MOST = 10
SPARE = 4
LANES = 128
F32 = jnp.float32
BF16 = jnp.bfloat16
MESH = pl.DeviceIdType.MESH


def fits_kernel(mesh, inverse_blocks, lower_late):
    sizes = (mesh.shape["prow"], mesh.shape["pcol"])
    return (
        sizes == (GRID_ROWS, GRID_COLS)
        and lower_late.shape == (14, BLK // GRID_COLS, WIDTH)
        and inverse_blocks.shape == (14 * BLK, 7 * BLK)
    )


def turned(left, right):
    return lax.dot_general(left, right, (((0,), (0,)), ((), ())), preferred_element_type=F32)


def step_kernel(
    inverse_hbm, late_hbm, early_hbm, link_hbm, diag_hbm, structures_ref,
    panel_late_ref, diag_late_ref, panel_early_ref, cross_ref, diag_early_ref,
    inverse, late_ref, early_ref, link_ref, diag_ref, masked, columns, wide, product, from_y, to_z, from_z, summed,
    sums, sums_wide, plane_in, depth_in, totals,
    late_sem, early_sem, inverse_sem, link_sem, diag_sem, first_send, first_recv, core_send, core_recv, x_send, x_recv,
    relay_send, relay_recv, y_send, y_recv, z_send, z_recv,
    plane_send, plane_recv, depth_send, depth_recv, total_send, total_recv,
):
    row_id = lax.axis_index("prow")
    col_id = lax.axis_index("pcol")
    z_id = col_id // 2
    y_id = lax.rem(col_id, 2)
    blocks, rows, _ = late_ref.shape
    half = blocks // 2
    listed = structures_ref.shape[1]
    core_peer = row_id + 1 - 2 * lax.rem(row_id, 2)
    x_peer = lax.rem(row_id + 2, GRID_ROWS)

    late_copy = pltpu.make_async_copy(late_hbm, late_ref, late_sem)
    early_copy = pltpu.make_async_copy(early_hbm, early_ref, early_sem)
    inverse_copy = pltpu.make_async_copy(inverse_hbm, inverse, inverse_sem)
    link_copy = pltpu.make_async_copy(link_hbm, link_ref, link_sem)
    diag_copy = pltpu.make_async_copy(diag_hbm, diag_ref, diag_sem)
    for copy in (late_copy, early_copy, inverse_copy, link_copy, diag_copy):
        copy.start()

    barrier = pltpu.get_barrier_semaphore()
    for step in range(1, GRID_ROWS * GRID_COLS):
        other = lax.rem(row_id * GRID_COLS + col_id + step, GRID_ROWS * GRID_COLS)
        pl.semaphore_signal(
            barrier,
            inc=1,
            device_id=(other // GRID_COLS, lax.rem(other, GRID_COLS)),
            device_id_type=MESH,
        )

    hits = []
    for panel in range(2):
        entries = [structures_ref[panel, entry] - row_id * blocks for entry in range(listed)]
        panel_hits = []
        for block in range(blocks):
            hit = jnp.int32(0)
            for entry in entries:
                hit += (entry == block).astype(jnp.int32)
            panel_hits.append(hit)
        hits.append(panel_hits)

    late_copy.wait()
    early_copy.wait()
    for panel, source in enumerate((late_ref, early_ref)):
        for block in range(blocks):
            masked[block, :, panel * WIDTH : (panel + 1) * WIDTH] = (
                source[block].astype(F32) * hits[panel][block].astype(F32)
            ).astype(BF16)

    pl.semaphore_wait(barrier, GRID_ROWS * GRID_COLS - 1)

    def remote(source, target, send, recv, device):
        return pltpu.make_async_remote_copy(
            src_ref=source,
            dst_ref=target,
            send_sem=send,
            recv_sem=recv,
            device_id=device,
            device_id_type=MESH,
        )

    core_id = lax.rem(row_id, 2)
    x_id = row_id // 2

    def strip(panel, source, x_half):
        start = pl.multiple_of(panel * WIDTH + x_half * LANES, LANES)
        return columns.at[:, source, :, pl.ds(start, LANES)]

    def first_parts(panel, x_half, y_to):
        start = panel * WIDTH + x_half * LANES
        part = masked.at[y_to * half : (y_to + 1) * half, :, start : start + LANES]
        target = (x_half * 2 + lax.rem(y_id + panel, 2), row_id * 2 + y_to)
        at_self = (row_id == target[0]) & (col_id == target[1])
        return part, strip(panel, col_id, x_half), target, at_self

    def first_copy(panel, x_half, y_to):
        part, to, target, _ = first_parts(panel, x_half, y_to)
        send = first_send.at[panel * 4 + x_half * 2 + y_to]
        return remote(part, to, send, first_recv.at[panel * DEPTH + z_id], target)

    def own_copy(panel, x_half, y_to):
        part, to, _, _ = first_parts(panel, x_half, y_to)
        return pltpu.make_async_copy(part, to, first_recv.at[panel * DEPTH + z_id])

    def is_self(panel, x_half, y_to):
        return first_parts(panel, x_half, y_to)[3]

    first_cases = [(p, x, y) for p in range(2) for x in range(2) for y in range(2)]
    for case in first_cases:
        pl.when(jnp.logical_not(is_self(*case)))(first_copy(*case).start)
        pl.when(is_self(*case))(own_copy(*case).start)

    def here(panel, index):
        return index * 2 + lax.rem(core_id + panel, 2)

    def there(panel, index):
        return index * 2 + lax.rem(core_id + panel + 1, 2)

    def core_copy(panel, index):
        part, at = strip(panel, here(panel, index), x_id), panel * DEPTH + index
        return remote(part, part, core_send.at[at], core_recv.at[at], (core_peer, col_id))

    def x_copy(panel, index):
        part, at = strip(panel, here(panel, index), x_id), panel * DEPTH + index
        return remote(part, part, x_send.at[at], x_recv.at[at], (x_peer, col_id))

    def relay_copy(panel, index):
        part, at = strip(panel, here(panel, index), 1 - x_id), panel * DEPTH + index
        return remote(part, part, relay_send.at[at], relay_recv.at[at], (core_peer, col_id))

    def arrived(part, sem):
        pltpu.make_async_copy(part, part, sem).wait()

    def spread(panel):
        for index in range(DEPTH):
            arrived(strip(panel, here(panel, index), x_id), first_recv.at[panel * DEPTH + index])
            x_copy(panel, index).start()
            core_copy(panel, index).start()

    def relay(panel):
        for index in range(DEPTH):
            arrived(strip(panel, here(panel, index), 1 - x_id), x_recv.at[panel * DEPTH + index])
            relay_copy(panel, index).start()

    def collect(panel):
        for index in range(DEPTH):
            at = panel * DEPTH + index
            arrived(strip(panel, there(panel, index), x_id), core_recv.at[at])
            arrived(strip(panel, there(panel, index), 1 - x_id), relay_recv.at[at])

    kept, dropped = [], []
    for panel in range(2):
        unlisted = jnp.int32(0)
        panel_kept, panel_dropped = [], []
        for block in range(blocks):
            drop = (1 - hits[panel][block]) * (unlisted < SPARE).astype(jnp.int32)
            panel_kept.append(1 - drop)
            panel_dropped.append(jnp.minimum(unlisted, SPARE))
            unlisted += 1 - hits[panel][block]
        kept.append(panel_kept)
        dropped.append(panel_dropped)

    def weight(panel, block, shift):
        same = (dropped[panel][block] == shift).astype(jnp.int32)
        return (same * kept[panel][block]).astype(F32)

    def placed(panel, block):
        parts = [
            weight(panel, block, shift) * summed[panel, block - shift]
            for shift in range(SPARE + 1)
            if 0 <= block - shift < MOST
        ]
        return functools.reduce(jnp.add, parts)

    def y_copy(panel, step):
        z_to = lax.rem(z_id + step, DEPTH)
        return remote(
            product.at[panel, :, z_to * 2 + 1 - y_id],
            from_y.at[panel, step],
            y_send.at[panel * DEPTH + step],
            y_recv.at[panel * DEPTH + step],
            (row_id, z_id * 2 + 1 - y_id),
        )

    def z_copy(panel, step):
        z_to = lax.rem(z_id + step, DEPTH)
        return remote(
            to_z.at[panel, step],
            from_z.at[panel, step],
            z_send.at[panel * DEPTH + step],
            z_recv.at[panel * DEPTH + step],
            (row_id, z_to * 2 + y_id),
        )

    order = (1, 2, 3, 0)

    def multiply(panel):
        right = columns[:, :, :, panel * WIDTH : (panel + 1) * WIDTH].reshape(-1, WIDTH)
        for start in range(0, blocks * BLK, 2 * BLK):
            wide[start : start + 2 * BLK] = jnp.dot(
                inverse[start : start + 2 * BLK], right, preferred_element_type=F32
            )
        for slot in range(MOST):
            chosen = functools.reduce(
                jnp.add,
                [
                    weight(panel, slot + shift, shift)
                    * wide[(slot + shift) * BLK : (slot + shift + 1) * BLK]
                    for shift in range(SPARE + 1)
                ],
            )
            product[panel, slot] = chosen.astype(BF16).reshape(GRID_COLS, rows, WIDTH)
        for step in order:
            y_copy(panel, step).start()

    def forward(panel, step):
        y_copy(panel, step).wait_recv()
        z_to = lax.rem(z_id + step, DEPTH)
        to_z[panel, step] = (
            product[panel, :, z_to * 2 + y_id].astype(F32) + from_y[panel, step].astype(F32)
        ).astype(BF16)
        z_copy(panel, step).start()

    def finish(panel):
        y_copy(panel, 0).wait_recv()
        total = product[panel, :, z_id * 2 + y_id].astype(F32) + from_y[panel, 0].astype(F32)
        for step in range(1, DEPTH):
            z_copy(panel, step).wait_recv()
            total += from_z[panel, step].astype(F32)
        summed[panel] = total

    place_id = row_id * 2 + y_id
    peers = GRID_ROWS * 2
    piece = (2 * WIDTH // peers, WIDTH // peers)
    base = (0, 2 * WIDTH)

    def plane_device(step):
        other = lax.rem(place_id + step, peers)
        return other, (other // 2, z_id * 2 + lax.rem(other, 2))

    def part_of(stage, index):
        size = piece[stage]
        return pl.ds(pl.multiple_of(base[stage] + index * size, size), size)

    def plane_copy(stage, step):
        other, device = plane_device(step)
        return remote(
            sums.at[part_of(stage, other)],
            plane_in.at[step, base[stage] // peers : base[stage] // peers + piece[stage]],
            plane_send.at[stage * peers + step],
            plane_recv.at[stage * peers + step],
            device,
        )

    def depth_copy(stage, step):
        z_to = lax.rem(z_id + step, DEPTH)
        part = depth_in.at[z_id, base[stage] // peers : base[stage] // peers + piece[stage]]
        return remote(
            part,
            part,
            depth_send.at[stage * DEPTH + step],
            depth_recv.at[stage * DEPTH + step],
            (row_id, z_to * 2 + y_id),
        )

    def total_copy(stage, step):
        _, device = plane_device(step)
        part = totals.at[part_of(stage, place_id)]
        return remote(
            part,
            part,
            total_send.at[stage * peers + step],
            total_recv.at[stage * peers + step],
            device,
        )

    def store_sums(stage, value, at):
        sums_wide[at : at + WIDTH] = value
        sums[at : at + WIDTH] = value.astype(BF16)

    def plane_sum(stage):
        start = base[stage] // peers
        total = sums_wide[part_of(stage, place_id)]
        for step in range(1, peers):
            plane_copy(stage, step).wait_recv()
            total += plane_in[step, start : start + piece[stage]].astype(F32)
        depth_in[z_id, start : start + piece[stage]] = total.astype(BF16)
        for step in range(1, DEPTH):
            depth_copy(stage, step).start()

    def depth_sum(stage):
        start = base[stage] // peers
        for step in range(1, DEPTH):
            source = lax.rem(z_id + DEPTH - step, DEPTH)
            arrived(
                depth_in.at[source, start : start + piece[stage]],
                depth_recv.at[stage * DEPTH + step],
            )
        total = depth_in[0, start : start + piece[stage]].astype(F32)
        for source in range(1, DEPTH):
            total += depth_in[source, start : start + piece[stage]].astype(F32)
        totals[part_of(stage, place_id)] = total.astype(BF16)
        for step in range(1, peers):
            total_copy(stage, step).start()

    def gather_totals(stage):
        for step in range(1, peers):
            source = lax.rem(place_id + peers - step, peers)
            arrived(totals.at[part_of(stage, source)], total_recv.at[stage * peers + step])

    link_copy.wait()
    diag_copy.wait()
    link = link_ref[...]
    late_rows = masked[:, :, :WIDTH].reshape(-1, WIDTH)
    early_rows = masked[:, :, WIDTH:].reshape(-1, WIDTH)

    spread(0)
    relay(0)
    collect(0)
    inverse_copy.wait()
    multiply(0)
    spread(1)
    forward(0, 1)
    relay(1)
    forward(0, 2)
    collect(1)
    multiply(1)
    forward(0, 3)
    for step in order[:-1]:
        forward(1, step)

    finish(0)
    for block in range(blocks):
        panel_late_ref[block] = -(placed(0, block) * hits[0][block].astype(F32))
    late_flat = panel_late_ref[...].reshape(-1, WIDTH)
    upper, lower = split_parts(late_flat)
    store_sums(0, turned(late_rows, upper) + turned(late_rows, lower), 0)
    store_sums(0, turned(upper, early_rows) + turned(lower, early_rows), WIDTH)
    for step in range(1, peers):
        plane_copy(0, step).start()
    carried = jnp.dot(upper, link, preferred_element_type=F32) + jnp.dot(
        lower, link, preferred_element_type=F32
    )
    carried = carried.reshape(blocks, rows, WIDTH)

    plane_sum(0)

    finish(1)
    for block in range(blocks):
        panel_early_ref[block] = -(
            (placed(1, block) + carried[block]) * hits[1][block].astype(F32)
        )
    early_upper, early_lower = split_parts(panel_early_ref[...].reshape(-1, WIDTH))
    store_sums(1, turned(early_rows, early_upper) + turned(early_rows, early_lower), 2 * WIDTH)
    for step in range(1, peers):
        plane_copy(1, step).start()

    depth_sum(0)
    plane_sum(1)
    depth_sum(1)
    gather_totals(0)
    diag_late = diag_ref[0] - totals[:WIDTH].astype(F32)
    diag_late_ref[...] = diag_late
    upper, lower = split_parts(diag_late)
    cross = (
        -totals[WIDTH : 2 * WIDTH].astype(F32)
        - jnp.dot(upper, link, preferred_element_type=F32)
        - jnp.dot(lower, link, preferred_element_type=F32)
    )
    cross_ref[...] = cross
    upper, lower = split_parts(cross)
    carried = turned(link, upper) + turned(link, lower)
    gather_totals(1)
    diag_early_ref[...] = diag_ref[1] - totals[2 * WIDTH :].astype(F32) - carried

    for case in first_cases:
        pl.when(jnp.logical_not(is_self(*case)))(first_copy(*case).wait_send)
    for panel in range(2):
        for index in range(DEPTH):
            x_copy(panel, index).wait_send()
            core_copy(panel, index).wait_send()
            relay_copy(panel, index).wait_send()
    for panel in range(2):
        for step in range(DEPTH):
            y_copy(panel, step).wait_send()
        for step in range(1, DEPTH):
            z_copy(panel, step).wait_send()
            depth_copy(panel, step).wait_send()
        for step in range(1, peers):
            plane_copy(panel, step).wait_send()
            total_copy(panel, step).wait_send()


def kernel_shards(inverse_blocks, lower_late, lower_early, link_block, diag_inverse, structures):
    blocks, rows, _ = lower_late.shape
    dma = pltpu.SemaphoreType.DMA
    vmem = pl.BlockSpec(memory_space=pltpu.VMEM)
    square = jax.ShapeDtypeStruct((WIDTH, WIDTH), F32)
    panel = jax.ShapeDtypeStruct(lower_late.shape, F32)
    peers = GRID_ROWS * 2
    sized = pltpu.VMEM
    return pl.pallas_call(
        step_kernel,
        out_shape=(panel, square, panel, square, square),
        in_specs=[
            *(pl.BlockSpec(memory_space=pl.ANY),) * 5,
            pl.BlockSpec(memory_space=pltpu.SMEM),
        ],
        out_specs=(vmem,) * 5,
        scratch_shapes=[
            sized(inverse_blocks.shape, BF16),
            sized(lower_late.shape, BF16),
            sized(lower_early.shape, BF16),
            sized(link_block.shape, BF16),
            sized(diag_inverse.shape, F32),
            sized((blocks, rows, 2 * WIDTH), BF16),
            sized((blocks // 2, GRID_COLS, rows, 2 * WIDTH), BF16),
            sized((blocks * BLK, WIDTH), F32),
            sized((2, MOST, GRID_COLS, rows, WIDTH), BF16),
            sized((2, DEPTH, MOST, rows, WIDTH), BF16),
            sized((2, DEPTH, MOST, rows, WIDTH), BF16),
            sized((2, DEPTH, MOST, rows, WIDTH), BF16),
            sized((2, MOST, rows, WIDTH), F32),
            sized((3 * WIDTH, WIDTH), BF16),
            sized((3 * WIDTH, WIDTH), F32),
            sized((peers, 3 * WIDTH // peers, WIDTH), BF16),
            sized((DEPTH, 3 * WIDTH // peers, WIDTH), BF16),
            sized((3 * WIDTH, WIDTH), BF16),
            dma,
            dma,
            dma,
            dma,
            dma,
            dma((GRID_ROWS * 2,)),
            dma((GRID_COLS,)),
            dma((GRID_COLS,)),
            dma((GRID_COLS,)),
            dma((GRID_COLS,)),
            dma((GRID_COLS,)),
            dma((GRID_COLS,)),
            dma((GRID_COLS,)),
            dma((2 * DEPTH,)),
            dma((2 * DEPTH,)),
            dma((2 * DEPTH,)),
            dma((2 * DEPTH,)),
            dma((2 * peers,)),
            dma((2 * peers,)),
            dma((2 * DEPTH,)),
            dma((2 * DEPTH,)),
            dma((2 * peers,)),
            dma((2 * peers,)),
        ],
        compiler_params=pltpu.CompilerParams(
            collective_id=0, has_side_effects=True, vmem_limit_bytes=52 * 1024 * 1024
        ),
    )(inverse_blocks, lower_late, lower_early, link_block, diag_inverse, structures)


def solution(mesh):
    placed = (P("prow", "pcol"), P("prow", "pcol", None), P("prow", "pcol", None), P(), P(), P())

    def shards(inverse_blocks, lower_late, *others):
        if fits_kernel(mesh, inverse_blocks, lower_late):
            return kernel_shards(inverse_blocks, lower_late, *others)
        return plain_shards(inverse_blocks, lower_late, *others)

    return jax.shard_map(
        shards,
        mesh=mesh,
        in_specs=placed,
        out_specs=(P("prow", "pcol", None), P(), P("prow", "pcol", None), P(), P()),
        check_vma=False,
    )
```
